32 devices in a mesh: groups: 2 (over x), cuts: 16 (over z, y, core).
Axes of the slice: x: 2, y: 2, z: 4, core: 2. Of those that a mesh axis runs over, the one named last changes fastest.
Arguments:
- displacement: float32 [2, 5, 5, 5, 32, 256], P(None, None, None, None, ('groups', 'cuts')), parts along dimension 4, may hold values from -6 to 6
- velocity: float32 [2, 5, 5, 5, 32, 256], P(None, None, None, None, ('groups', 'cuts')), parts along dimension 4, may hold values from -6 to 6
- modulus: float32 [32, 256], P(('groups', 'cuts')), parts along dimension 0, may hold values from 0.5 to 2
- density: float32 [32, 256], P(('groups', 'cuts')), parts along dimension 0, may hold values from 0.5 to 2
- adjoint_source: float32 [5, 5, 5, 32, 256], P(None, None, None, ('groups', 'cuts')), parts along dimension 3, may hold values from -6 to 6
- database: float32 [16384, 100], P(('groups', 'cuts')), parts along dimension 0, may hold values from -24 to 24
- face_source: int32 [2048, 1], P(('groups', 'cuts')), parts along dimension 0, may hold values from 0 to 15; in each aligned block of 64 rows (0 to 63, 64 to 127, ...) at most 16 rows name the same one
- face_slot: int32 [2048], P(('groups', 'cuts')), parts along dimension 0, may hold values from 0 to 511
Outputs:
- new_displacement: float32 [2, 5, 5, 5, 32, 256], P(None, None, None, None, ('groups', 'cuts')), parts along dimension 4
- new_velocity: float32 [2, 5, 5, 5, 32, 256], P(None, None, None, None, ('groups', 'cuts')), parts along dimension 4
- kernel: float32 [5, 5, 5, 32, 256], P(None, None, None, ('groups', 'cuts')), parts along dimension 3
The draws below stay inside these ranges and needn't reach their ends.
There are 2 independent parts, one for each index of `groups`. The reference program is written for one: setup_inputs(seed, part) draws one part's arguments, and reference() takes and returns one part's arrays. A program takes and returns all parts, laid end to end along the dimension named above; each array names one. Nothing has to cross between parts.
Inputs may be any that keep to these rules, and one draw needn't show every extreme that they name: `face_source`: no more than 16 faces of one slab name the same source, a bound that some block reaches.
All inputs are finite; a program needn't handle non-finite values.
Results may differ from the reference program's by a relative error of at most 0.0001.
Values sent between devices are 32-bit elements; how exact they have to be, the bound alone decides.
A program may use at most 64 MiB of HBM per device.

```python
import math
import jax
import jax.numpy as jnp
import numpy as np
from jax import lax

EDGE = 16
EZ_DEV = 1
STEPS = 4
RECS_DEV = 512
EZT = 16
EXY = 256
FACES_DEV = 64
FACES = 1024
RECS = 8192
CAP = 16
N_CUTS = 16


def place_ends(values, key, low, top_value):
    extent = values.shape
    place = [jax.random.randint(jax.random.fold_in(key, axis), (), 0, extent[axis]) for axis in range(len(extent))]
    values = values.at[tuple(place)].set(low)
    longest = extent.index(max(extent))
    place[longest] = (place[longest] + 1) % extent[longest]
    return values.at[tuple(place)].set(top_value)


def shard_levels(stream_key, extent, pieces, least, high):
    gain = 1.0
    for axis_at, shards_of in pieces:
        steps = jax.random.uniform(jax.random.fold_in(jax.random.fold_in(stream_key, 6), axis_at), (shards_of,), jnp.float32, least / len(pieces), high / len(pieces))
        gain = gain * jnp.repeat(jnp.exp(steps), extent[axis_at] // shards_of).reshape((-1,) + (1,) * (len(extent) - 1 - axis_at))
    return gain


def routed_block(own_key, own, number, rows, count, top, bound, skew):
    sequence = jax.random.permutation(own_key, count)
    packed, usual = portions_of(count, rows * top, bound, skew, True), portions_of(count, rows * top, bound, skew, False)
    places = jnp.arange(count)

    def named(tallies, offset_by):
        used = int((tallies > 0).sum())
        fixed = max(1, used // 4)
        passed = fixed + (places - fixed + offset_by * (used - fixed)) % max(1, count - fixed)
        return jnp.zeros((count,), jnp.int32).at[sequence[jnp.where(places < fixed, places, passed)]].set(jnp.asarray(tallies, jnp.int32))

    tallies = jnp.where(number % 4 == 0, named(packed, number // 4), named(usual, number - number // 4 - 1))
    mixed = jax.random.permutation(jax.random.fold_in(own, 3), count)
    donor, sink = mixed[0:count // 2 * 2:2], mixed[1:count // 2 * 2:2]
    slack = jnp.minimum(tallies[donor] - 1, bound - tallies[sink]) // 2
    slack = jnp.where((donor == sequence[0]) | (sink == sequence[0]) | (tallies[sink] == 0), 0, jnp.maximum(slack, 0))
    passed = jax.random.randint(jax.random.fold_in(own, 4), (count // 2,), 0, 1 << 20) % (slack + 1)
    tallies = tallies.at[donor].add(-passed).at[sink].add(passed)
    members = jnp.searchsorted(jnp.cumsum(tallies), jnp.arange(rows * top), side="right").astype(jnp.int32)
    listing = members.reshape(top, rows).T
    listing = listing[jax.random.permutation(jax.random.fold_in(own, 1), rows)]
    offset_by = jax.random.randint(jax.random.fold_in(own, 2), (rows, 1), 0, top)
    return jnp.take_along_axis(listing, (jnp.arange(top)[None, :] + offset_by) % top, axis=1)


def portions_of(count, total, most, slope, full):
    portions = [(1 << 20) // math.isqrt(standing ** slope) + 1 for standing in range(1, count + 1)]
    largest = most if full else min(most, max(-(-total // count), total * portions[0] // sum(portions)))
    least = 1 if total - largest >= count - 1 else 0
    counts, spare = [largest] + [least] * (count - 1), total - largest - least * (count - 1)
    while spare > 0:
        candidates = [i for i in range(1, count) if counts[i] < largest] or [i for i in range(1, count) if counts[i] < most]
        whole, left = sum([portions[i] for i in candidates]), spare
        for i in candidates:
            extra = min(most - counts[i], max(1, left * portions[i] // whole), spare)
            counts[i] = counts[i] + extra
            spare = spare - extra
    return np.array(counts)


def bell_draw(key, shape, scale, reach, pieces=(), kind=jnp.bfloat16):
    level = shard_levels(key, shape, pieces, -0.22, 0.18) if pieces else 1.0
    drawn = jax.random.normal(key, shape, jnp.float32) * scale * level
    return jnp.minimum(jnp.maximum(drawn, -reach), reach).astype(kind)


def setup_inputs(seed: int = 0, part: int = 0) -> dict:
    splits = jax.random.split(jax.random.key(seed), 9)
    part_splits = jax.random.split(jax.random.fold_in(splits[8], part), 9)
    displacement = bell_draw(part_splits[0], (2, 5, 5, 5, EZT, EXY), 1.0, 6.0, ((4, 16),), jnp.float32)
    velocity = bell_draw(part_splits[1], (2, 5, 5, 5, EZT, EXY), 1.0, 6.0, ((4, 16),), jnp.float32)
    modulus = jnp.clip(jnp.exp(math.log(2.0) - 1.3862944 * jax.random.uniform(part_splits[2], (EZT, EXY), jnp.float32) ** shard_levels(part_splits[2], (EZT, EXY), ((0, 16),), -0.2, 0.2)), 0.5, 2.0)
    density = jnp.clip(jnp.exp(math.log(2.0) - 1.3862944 * jax.random.uniform(part_splits[3], (EZT, EXY), jnp.float32) ** shard_levels(part_splits[3], (EZT, EXY), ((0, 16),), -0.2, 0.2)), 0.5, 2.0)
    adjoint_source = bell_draw(part_splits[4], (5, 5, 5, EZT, EXY), 1.0, 6.0, ((3, 16),), jnp.float32)
    database = bell_draw(part_splits[5], (RECS, STEPS * 25), 4.0, 24.0, ((0, 16),), jnp.float32)
    face_source_keys = jax.random.split(jax.random.fold_in(part_splits[6], 1), FACES // FACES_DEV)
    face_source_turns = jax.random.permutation(jax.random.fold_in(part_splits[6], 3), FACES // FACES_DEV)
    face_source = jax.vmap(lambda own, number: routed_block(jax.random.fold_in(part_splits[6], 2), own, number, FACES_DEV, N_CUTS, 1, CAP, 2))(face_source_keys, face_source_turns).reshape((FACES, 1))
    face_slot = place_ends(jax.random.randint(part_splits[7], (FACES,), 0, RECS_DEV), jax.random.fold_in(part_splits[7], 1), 0, RECS_DEV - 1).astype(jnp.int32)
    return dict(displacement=displacement, velocity=velocity, modulus=modulus, density=density, adjoint_source=adjoint_source, database=database, face_source=face_source, face_slot=face_slot)


TIME_STEP = 0.03

def gll_tables():
    points = np.array([-1.0, -math.sqrt(3.0 / 7.0), 0.0, math.sqrt(3.0 / 7.0), 1.0])
    weights = np.array([0.1, 49.0 / 90.0, 32.0 / 45.0, 49.0 / 90.0, 0.1])
    derivative = np.zeros((5, 5))
    for node_row in range(5):
        for node_col in range(5):
            summed = 0.0
            for other_node in range(5):
                if other_node == node_col:
                    continue
                term = 1.0 / (points[node_col] - points[other_node])
                for third_node in range(5):
                    if third_node != node_col and third_node != other_node:
                        term = term * (points[node_row] - points[third_node]) / (points[node_col] - points[third_node])
                summed = summed + term
            derivative[node_row, node_col] = summed
    return (derivative, weights)

def stiffness(fields, modulus, derivative, weights_cube):
    highest = lax.Precision.HIGHEST
    grad_z = jnp.einsum('ak,fkbcze->fabcze', derivative, fields, precision=highest)
    grad_y = jnp.einsum('bk,fakcze->fabcze', derivative, fields, precision=highest)
    grad_x = jnp.einsum('ck,fabkze->fabcze', derivative, fields, precision=highest)
    scaled = weights_cube[:, :, :, None, None] * modulus[None, None, None]
    action = jnp.einsum('ak,fabcze->fkbcze', derivative, grad_z * scaled, precision=highest)
    action = action + jnp.einsum('bk,fabcze->fakcze', derivative, grad_y * scaled, precision=highest)
    action = action + jnp.einsum('ck,fabcze->fabkze', derivative, grad_x * scaled, precision=highest)
    return (action, grad_z, grad_y, grad_x)

def plane_assemble(values, edge):
    count = values.shape[-1]
    column = jnp.arange(count) % edge
    line = jnp.arange(count) // edge
    first = values[:, :, :, 0]
    last = values[:, :, :, 4]
    from_right = jnp.where(column != edge - 1, jnp.roll(first, -1, axis=-1), 0.0)
    from_left = jnp.where(column != 0, jnp.roll(last, 1, axis=-1), 0.0)
    values = jnp.concatenate([(first + from_left)[:, :, :, None], values[:, :, :, 1:4], (last + from_right)[:, :, :, None]], axis=3)
    first = values[:, :, 0]
    last = values[:, :, 4]
    from_right = jnp.where(line != edge - 1, jnp.roll(first, -edge, axis=-1), 0.0)
    from_left = jnp.where(line != 0, jnp.roll(last, edge, axis=-1), 0.0)
    return jnp.concatenate([(first + from_left)[:, :, None], values[:, :, 1:4], (last + from_right)[:, :, None]], axis=2)

def join_layers(values, below, above):
    first = values[:, 0]
    last = values[:, 4]
    from_under = jnp.concatenate([below[:, :, :, None], last[:, :, :, :-1]], axis=3)
    from_over = jnp.concatenate([first[:, :, :, 1:], above[:, :, :, None]], axis=3)
    return jnp.concatenate([(first + from_under)[:, None], values[:, 1:4], (last + from_over)[:, None]], axis=1)

def face_force(traction, layer_count, edge, weights):
    face_weight = weights[:, None] * weights[None, :]
    sides = traction.reshape(4, layer_count, edge, 5, 5) * face_weight
    sides = jnp.transpose(sides, (0, 3, 4, 1, 2))
    force = jnp.zeros((5, 5, 5, layer_count, edge, edge), jnp.float32)
    force = force.at[:, :, 0, :, :, 0].add(sides[0])
    force = force.at[:, :, 4, :, :, edge - 1].add(sides[1])
    force = force.at[:, 0, :, :, 0, :].add(sides[2])
    force = force.at[:, 4, :, :, edge - 1, :].add(sides[3])
    return force.reshape(5, 5, 5, layer_count, edge * edge)

def full_assemble(values, edge):
    values = plane_assemble(values, edge)
    empty = jnp.zeros((values.shape[0], 5, 5, values.shape[-1]), jnp.float32)
    return join_layers(values, empty, empty)

def reference(displacement, velocity, modulus, density, adjoint_source, database, face_source, face_slot):
    derivative_np, weights_np = gll_tables()
    derivative = jnp.asarray(derivative_np, dtype=jnp.float32)
    weights = jnp.asarray(weights_np, dtype=jnp.float32)
    weights_cube = weights[:, None, None] * weights[None, :, None] * weights[None, None, :]
    layer_count = displacement.shape[4]
    mass = full_assemble((density[None, None, None] * weights_cube[:, :, :, None, None])[None], EDGE)
    inverse_mass = 1.0 / mass
    record = face_source[:, 0] * RECS_DEV + face_slot
    records = database[record].reshape(N_CUTS, 4, EZ_DEV, EDGE, STEPS, 25)
    records = jnp.transpose(records, (1, 0, 2, 3, 4, 5)).reshape(4 * layer_count * EDGE, STEPS, 25)
    kernel = jnp.zeros(adjoint_source.shape, jnp.float32)
    for step in range(STEPS):
        action, grad_z, grad_y, grad_x = stiffness(displacement, modulus, derivative, weights_cube)
        product = grad_z[0] * grad_z[1] + grad_y[0] * grad_y[1] + grad_x[0] * grad_x[1]
        kernel = kernel - TIME_STEP * modulus[None, None, None] * product
        force = jnp.stack([face_force(records[:, step], layer_count, EDGE, weights), adjoint_source])
        accel = full_assemble(force - action, EDGE) * inverse_mass
        velocity = velocity + TIME_STEP * accel
        displacement = displacement + TIME_STEP * velocity
    return (displacement, velocity, kernel)
```

```python
import functools
import math

import jax
import jax.numpy as jnp
import numpy as np
from jax import lax
from jax.experimental import pallas as pl
from jax.experimental.pallas import tpu as pltpu
from jax.sharding import PartitionSpec as P

EDGE = 16
STEPS = 4
TIME_STEP = 0.03
MESH = pl.DeviceIdType.MESH


def gll_tables():
    points = np.array([-1.0, -math.sqrt(3.0 / 7.0), 0.0, math.sqrt(3.0 / 7.0), 1.0])
    weights = np.array([0.1, 49.0 / 90.0, 32.0 / 45.0, 49.0 / 90.0, 0.1])
    derivative = np.zeros((5, 5))
    for node_row in range(5):
        for node_col in range(5):
            summed = 0.0
            for other_node in range(5):
                if other_node == node_col:
                    continue
                term = 1.0 / (points[node_col] - points[other_node])
                for third_node in range(5):
                    if third_node != node_col and third_node != other_node:
                        term = (
                            term
                            * (points[node_row] - points[third_node])
                            / (points[node_col] - points[third_node])
                        )
                summed = summed + term
            derivative[node_row, node_col] = summed
    return (derivative, weights)


DERIV, WEIGHTS = gll_tables()
STIFF = DERIV.T @ np.diag(WEIGHTS) @ DERIV
STIFF_W = STIFF / WEIGHTS[:, None]


def mix(row, parts):
    total = None
    for coefficient, part in zip(row, parts):
        if abs(coefficient) < 1e-12:
            continue
        term = float(coefficient) * part
        total = term if total is None else total + term
    return total


def iota(shape, dim):
    return lax.broadcasted_iota(jnp.int32, shape, dim)


def join_plane(plane):
    lane = iota((8, 128), 1)
    half = iota((8, 128), 0) % 2
    column = lane % EDGE
    first, last = plane[:, 0], plane[:, 4]
    from_left = jnp.where(column != 0, pltpu.roll(last, 1, 2), 0.0)
    from_right = jnp.where(column != EDGE - 1, pltpu.roll(first, 127, 2), 0.0)
    plane = jnp.concatenate(
        [(first + from_left)[:, None], plane[:, 1:4], (last + from_right)[:, None]], axis=1
    )
    first, last = plane[0], plane[4]
    rolled = pltpu.roll(last, EDGE, 2)
    under = jnp.where(half != 0, pltpu.roll(rolled, 1, 1), 0.0)
    from_left = jnp.where(lane < EDGE, under, rolled)
    rolled = pltpu.roll(first, 128 - EDGE, 2)
    over = jnp.where(half == 0, pltpu.roll(rolled, 7, 1), 0.0)
    from_right = jnp.where(lane >= 128 - EDGE, over, rolled)
    return jnp.concatenate(
        [(first + from_left)[None], plane[1:4], (last + from_right)[None]], axis=0
    )


def weighted(values):
    rows = [
        jnp.stack([float(WEIGHTS[b] * WEIGHTS[c]) * values for c in range(5)]) for b in range(5)
    ]
    return jnp.stack(rows)


def split(values):
    high = values.astype(jnp.bfloat16)
    low = (values - high.astype(jnp.float32)).astype(jnp.bfloat16)
    return high, low


def dot(left, right):
    return jnp.dot(left, right, preferred_element_type=jnp.float32)


def body_kernel(
    cuts,
    room,
    u_ref,
    v_ref,
    mod_ref,
    den_ref,
    adj_ref,
    db_ref,
    src_ref,
    slot_ref,
    u_out,
    v_out,
    k_out,
    disp,
    vel,
    inv,
    adj,
    ker,
    wmod,
    acc,
    records,
    req,
    req_in,
    rep,
    rep_in,
    den_in,
    face_out,
    face_in,
    req_send,
    req_recv,
    rep_send,
    rep_recv,
    den_send,
    den_recv,
    face_send,
    face_recv,
):
    group = lax.axis_index("groups")
    me = lax.axis_index("cuts")
    has_below = me > 0
    has_above = me < cuts - 1
    below = jnp.maximum(me - 1, 0)
    above = jnp.minimum(me + 1, cuts - 1)
    faces = src_ref.shape[0]
    table = db_ref.shape[0]

    barrier = pltpu.get_barrier_semaphore()

    def greet(k, carry):
        pl.semaphore_signal(
            barrier, inc=1, device_id=(group, lax.rem(me + k, cuts)), device_id_type=MESH
        )
        return carry

    lax.fori_loop(1, cuts, greet, 0)

    target_col = src_ref[...]
    slot_row = slot_ref[...]
    eye = iota((faces, faces), 0) == iota((faces, faces), 1)
    target_row = jnp.sum(jnp.where(eye, target_col, 0), axis=0, keepdims=True)
    same = target_col == target_row
    row_id, col_id = iota((faces, faces), 0), iota((faces, faces), 1)
    rank_row = jnp.sum(jnp.where(same & (row_id < col_id), 1, 0), axis=0, keepdims=True)
    rank_col = jnp.sum(jnp.where(same & (col_id < row_id), 1, 0), axis=1, keepdims=True)
    place_row = target_row * room + rank_row
    place_col = target_col * room + rank_col
    wanted = jnp.where(iota((cuts * room, faces), 0) == place_row, slot_row, 0)
    wanted = jnp.sum(wanted, axis=1, keepdims=True)
    req[...] = jnp.broadcast_to(wanted, (cuts * room, 128)).reshape(cuts, room, 128)

    @pl.when(jnp.logical_not(has_below))
    def _():
        face_in[:, 0] = jnp.zeros((STEPS, 25, 4, 128), jnp.float32)
        den_in[0] = jnp.zeros((2, 128), jnp.float32)

    @pl.when(jnp.logical_not(has_above))
    def _():
        face_in[:, 1] = jnp.zeros((STEPS, 25, 4, 128), jnp.float32)
        den_in[1] = jnp.zeros((2, 128), jnp.float32)

    pl.semaphore_wait(barrier, cuts - 1)

    def req_copy(k):
        peer = lax.rem(me + k, cuts)
        return pltpu.make_async_remote_copy(
            src_ref=req.at[peer],
            dst_ref=req_in.at[me],
            send_sem=req_send.at[k],
            recv_sem=req_recv.at[k],
            device_id=(group, peer),
            device_id_type=MESH,
        )

    def rep_copy(k):
        peer = lax.rem(me + k, cuts)
        return pltpu.make_async_remote_copy(
            src_ref=rep.at[peer],
            dst_ref=rep_in.at[me],
            send_sem=rep_send.at[k],
            recv_sem=rep_recv.at[k],
            device_id=(group, peer),
            device_id_type=MESH,
        )

    def den_copy(up):
        return pltpu.make_async_remote_copy(
            src_ref=den_ref,
            dst_ref=den_in.at[1 - up],
            send_sem=den_send.at[up],
            recv_sem=den_recv.at[up],
            device_id=(group, above if up else below),
            device_id_type=MESH,
        )

    def face_copy(step, up):
        return pltpu.make_async_remote_copy(
            src_ref=face_out.at[step, up],
            dst_ref=face_in.at[step, 1 - up],
            send_sem=face_send.at[step, up],
            recv_sem=face_recv.at[step, up],
            device_id=(group, above if up else below),
            device_id_type=MESH,
        )

    def start_all(make):
        def go(k, carry):
            make(k).start()
            return carry

        lax.fori_loop(1, cuts, go, 0)

    def wait_all(make):
        def go(k, carry):
            copy = make(k)
            copy.wait_send()
            copy.wait_recv()
            return carry

        lax.fori_loop(1, cuts, go, 0)

    start_all(req_copy)

    @pl.when(has_above)
    def _():
        den_copy(1).start()

    @pl.when(has_below)
    def _():
        den_copy(0).start()

    req_in[pl.ds(me, 1)] = req[pl.ds(me, 1)]

    blank = jnp.zeros((125, 8, 128), jnp.float32)
    disp[...] = blank
    vel[...] = blank
    adj[...] = blank
    ker[...] = blank
    disp[:, 0:2, :] = u_ref[0]
    disp[:, 2:4, :] = u_ref[1]
    vel[:, 0:2, :] = v_ref[0]
    vel[:, 2:4, :] = v_ref[1]
    adj[:, 2:4, :] = adj_ref[...]
    modulus = jnp.concatenate([mod_ref[...]] * 4, axis=0)
    density = jnp.concatenate([den_ref[...]] * 4, axis=0)
    wmod[...] = weighted(modulus).reshape(25, 8, 128)
    records[...] = jnp.zeros_like(records)
    high, low = split(db_ref[...])

    wait_all(req_copy)
    asked = req_in[...].reshape(cuts * room, 128)
    pick = jnp.concatenate(
        [
            jnp.where(asked == iota(asked.shape, 1) + at, 1.0, 0.0).astype(jnp.bfloat16)
            for at in range(0, table, 128)
        ],
        axis=1,
    )
    served = dot(pick, high) + dot(pick, low)
    rep[...] = jnp.zeros_like(rep)
    rep[:, :, 0 : served.shape[1]] = served.reshape(cuts, room, served.shape[1])
    start_all(rep_copy)
    rep_in[pl.ds(me, 1)] = rep[pl.ds(me, 1)]

    @pl.when(has_above)
    def _():
        den_copy(1).wait_send()

    @pl.when(has_below)
    def _():
        den_copy(0).wait_send()

    @pl.when(has_below)
    def _():
        den_copy(1).wait_recv()

    @pl.when(has_above)
    def _():
        den_copy(0).wait_recv()

    for a in range(5):
        if a in (0, 1, 4):
            near = density
            if a != 1:
                near = near + jnp.concatenate([den_in[a // 4]] * 4, axis=0)
            mass = join_plane(weighted(near)).reshape(25, 8, 128)
            base = TIME_STEP / mass
        inv[25 * a : 25 * a + 25] = float(1.0 / WEIGHTS[a]) * base

    node = iota((128, 1), 0) % 25

    def weight_of(index):
        return jnp.where(
            (index == 0) | (index == 4),
            float(WEIGHTS[0]),
            jnp.where(index == 2, float(WEIGHTS[2]), float(WEIGHTS[1])),
        )

    face_weight = weight_of(node // 5) * weight_of(node % 5)
    element = iota((faces, EDGE * EDGE), 1)
    face_id = iota((faces, EDGE * EDGE), 0)
    line, column = element // EDGE, element % EDGE
    spots = (
        (column == 0, line),
        (column == EDGE - 1, line),
        (line == 0, column),
        (line == EDGE - 1, column),
    )
    wait_all(rep_copy)
    got = jnp.transpose(rep_in[...].reshape(cuts * room, 128)) * face_weight
    got_high, got_low = split(got)
    for side, (here, along) in enumerate(spots):
        chosen = here & (face_id == along + side * EDGE)
        place = jnp.sum(jnp.where(chosen, place_col + 1, 0), axis=0, keepdims=True) - 1
        put = jnp.where(iota((cuts * room, EDGE * EDGE), 0) == place, 1.0, 0.0)
        put = put.astype(jnp.bfloat16)
        moved = dot(got_high, put) + dot(got_low, put)
        records[side, :, 0, :] = moved[:, 0:128]
        records[side, :, 1, :] = moved[:, 128:256]

    def plane_of(ref, a):
        return ref[25 * a : 25 * a + 25].reshape(5, 5, 8, 128)

    def residual(step, a):
        plane = plane_of(disp, a)
        total = mix(STIFF[a], [plane_of(disp, k) for k in range(5)])
        coupling = STIFF_W * WEIGHTS[a]
        total = total + jnp.stack([mix(coupling[b], [plane[k] for k in range(5)]) for b in range(5)])
        total = total + jnp.stack(
            [mix(coupling[c], [plane[:, k] for k in range(5)]) for c in range(5)], axis=1
        )
        force = plane_of(adj, a) - wmod[...].reshape(5, 5, 8, 128) * total
        at = pl.ds(25 * step + 5 * a, 5)
        force = jnp.concatenate(
            [
                (force[:, 0] + records[0, at])[:, None],
                force[:, 1:4],
                (force[:, 4] + records[1, at])[:, None],
            ],
            axis=1,
        )
        force = jnp.concatenate(
            [
                (force[0] + records[2, at])[None],
                force[1:4],
                (force[4] + records[3, at])[None],
            ],
            axis=0,
        )
        return join_plane(force).reshape(25, 8, 128)

    def advance(a, force):
        rows = slice(25 * a, 25 * a + 25)
        speed = vel[rows] + inv[rows] * force
        vel[rows] = speed
        disp[rows] = disp[rows] + TIME_STEP * speed

    def sensitivity(a):
        plane = plane_of(disp, a)
        total = 0.0
        for grad in (
            mix(DERIV[a], [plane_of(disp, k) for k in range(5)]),
            jnp.stack([mix(DERIV[b], [plane[k] for k in range(5)]) for b in range(5)]),
            jnp.stack([mix(DERIV[c], [plane[:, k] for k in range(5)]) for c in range(5)], axis=1),
        ):
            grad = grad.reshape(25, 8, 128)
            total = total + grad * pltpu.roll(grad, 6, 1)
        rows = slice(25 * a, 25 * a + 25)
        ker[rows] = ker[rows] + total

    def one_step(step, carry):
        for a in (4, 0):
            force = residual(step, a)
            acc[25 * a : 25 * a + 25] = force
            face_out[step, a // 4] = force[:, 0:4]
            if a:

                @pl.when(has_above)
                def _():
                    face_copy(step, 1).start()
            else:

                @pl.when(has_below)
                def _():
                    face_copy(step, 0).start()

        for a in (1, 2, 3):
            acc[25 * a : 25 * a + 25] = residual(step, a)
        for a in range(5):
            sensitivity(a)
        for a in (1, 2, 3):
            advance(a, acc[25 * a : 25 * a + 25])

        @pl.when(has_below)
        def _():
            face_copy(step, 1).wait_recv()

        @pl.when(has_above)
        def _():
            face_copy(step, 0).wait_recv()

        for a in (0, 4):
            other = face_in[step, a // 4]
            other = jnp.concatenate([other, jnp.zeros_like(other)], axis=1)
            advance(a, acc[25 * a : 25 * a + 25] + other)

        @pl.when(has_above)
        def _():
            face_copy(step, 1).wait_send()

        @pl.when(has_below)
        def _():
            face_copy(step, 0).wait_send()

        return carry

    lax.fori_loop(0, STEPS, one_step, 0)

    for field in range(2):
        u_out[field] = disp[:, 2 * field : 2 * field + 2, :]
        v_out[field] = vel[:, 2 * field : 2 * field + 2, :]
    k_out[...] = ker[:, 0:2, :] * (-TIME_STEP * mod_ref[...])


def body(
    displacement, velocity, modulus, density, adjoint_source, database, face_source, face_slot
):
    cuts = lax.axis_size("cuts")
    faces = face_source.shape[0]
    capacity = max(2, 4 * faces // cuts)
    room = -(-capacity // 8) * 8
    vmem = pl.BlockSpec(memory_space=pltpu.VMEM)
    f32 = jnp.float32
    dma = pltpu.SemaphoreType.DMA
    big = pltpu.VMEM((125, 8, 128), f32)
    out = pl.pallas_call(
        functools.partial(body_kernel, cuts, room),
        out_shape=(
            jax.ShapeDtypeStruct((2, 125, 2, 128), f32),
            jax.ShapeDtypeStruct((2, 125, 2, 128), f32),
            jax.ShapeDtypeStruct((125, 2, 128), f32),
        ),
        in_specs=[vmem] * 8,
        out_specs=(vmem, vmem, vmem),
        scratch_shapes=[
            big,
            big,
            big,
            big,
            big,
            pltpu.VMEM((25, 8, 128), f32),
            big,
            pltpu.VMEM((4, 128, 8, 128), f32),
            pltpu.VMEM((cuts, room, 128), jnp.int32),
            pltpu.VMEM((cuts, room, 128), jnp.int32),
            pltpu.VMEM((cuts, room, 128), f32),
            pltpu.VMEM((cuts, room, 128), f32),
            pltpu.VMEM((2, 2, 128), f32),
            pltpu.VMEM((STEPS, 2, 25, 4, 128), f32),
            pltpu.VMEM((STEPS, 2, 25, 4, 128), f32),
            dma((cuts,)),
            dma((cuts,)),
            dma((cuts,)),
            dma((cuts,)),
            dma((2,)),
            dma((2,)),
            dma((STEPS, 2)),
            dma((STEPS, 2)),
        ],
        compiler_params=pltpu.CompilerParams(
            collective_id=0, has_side_effects=True, vmem_limit_bytes=40 * 1024 * 1024
        ),
    )(
        displacement.reshape(2, 125, 2, 128),
        velocity.reshape(2, 125, 2, 128),
        modulus.reshape(2, 128),
        density.reshape(2, 128),
        adjoint_source.reshape(125, 2, 128),
        database,
        face_source,
        face_slot.reshape(1, faces),
    )
    return (
        out[0].reshape(displacement.shape),
        out[1].reshape(velocity.shape),
        out[2].reshape(adjoint_source.shape),
    )


def solution(mesh):
    return jax.shard_map(
        body,
        mesh=mesh,
        in_specs=(
            P(None, None, None, None, ("groups", "cuts"), None),
            P(None, None, None, None, ("groups", "cuts"), None),
            P(("groups", "cuts"), None),
            P(("groups", "cuts"), None),
            P(None, None, None, ("groups", "cuts"), None),
            P(("groups", "cuts"), None),
            P(("groups", "cuts"), None),
            P(("groups", "cuts")),
        ),
        out_specs=(
            P(None, None, None, None, ("groups", "cuts"), None),
            P(None, None, None, None, ("groups", "cuts"), None),
            P(None, None, None, ("groups", "cuts"), None),
        ),
        check_vma=False,
    )
```

```python
import functools
import math

import jax
import jax.numpy as jnp
import numpy as np
from jax import lax
from jax.experimental import pallas as pl
from jax.experimental.pallas import tpu as pltpu
from jax.sharding import PartitionSpec as P

EDGE = 16
STEPS = 4
TIME_STEP = 0.03
MESH = pl.DeviceIdType.MESH


def gll_tables():
    points = np.array([-1.0, -math.sqrt(3.0 / 7.0), 0.0, math.sqrt(3.0 / 7.0), 1.0])
    weights = np.array([0.1, 49.0 / 90.0, 32.0 / 45.0, 49.0 / 90.0, 0.1])
    derivative = np.zeros((5, 5))
    for node_row in range(5):
        for node_col in range(5):
            summed = 0.0
            for other_node in range(5):
                if other_node == node_col:
                    continue
                term = 1.0 / (points[node_col] - points[other_node])
                for third_node in range(5):
                    if third_node != node_col and third_node != other_node:
                        term = (
                            term
                            * (points[node_row] - points[third_node])
                            / (points[node_col] - points[third_node])
                        )
                summed = summed + term
            derivative[node_row, node_col] = summed
    return (derivative, weights)


DERIV, WEIGHTS = gll_tables()
STIFF = DERIV.T @ np.diag(WEIGHTS) @ DERIV
STIFF_W = STIFF / WEIGHTS[:, None]


def mix(row, parts):
    total = None
    for coefficient, part in zip(row, parts):
        if abs(coefficient) < 1e-12:
            continue
        term = float(coefficient) * part
        total = term if total is None else total + term
    return total


def iota(shape, dim):
    return lax.broadcasted_iota(jnp.int32, shape, dim)


def join_plane(plane):
    lane = iota((8, 128), 1)
    half = iota((8, 128), 0) % 2
    column = lane % EDGE
    first, last = plane[:, 0], plane[:, 4]
    from_left = jnp.where(column != 0, pltpu.roll(last, 1, 2), 0.0)
    from_right = jnp.where(column != EDGE - 1, pltpu.roll(first, 127, 2), 0.0)
    plane = jnp.concatenate(
        [(first + from_left)[:, None], plane[:, 1:4], (last + from_right)[:, None]], axis=1
    )
    first, last = plane[0], plane[4]
    rolled = pltpu.roll(last, EDGE, 2)
    under = jnp.where(half != 0, pltpu.roll(rolled, 1, 1), 0.0)
    from_left = jnp.where(lane < EDGE, under, rolled)
    rolled = pltpu.roll(first, 128 - EDGE, 2)
    over = jnp.where(half == 0, pltpu.roll(rolled, 7, 1), 0.0)
    from_right = jnp.where(lane >= 128 - EDGE, over, rolled)
    return jnp.concatenate(
        [(first + from_left)[None], plane[1:4], (last + from_right)[None]], axis=0
    )


def weighted(values):
    rows = [
        jnp.stack([float(WEIGHTS[b] * WEIGHTS[c]) * values for c in range(5)]) for b in range(5)
    ]
    return jnp.stack(rows)


def split(values):
    high = values.astype(jnp.bfloat16)
    low = (values - high.astype(jnp.float32)).astype(jnp.bfloat16)
    return high, low


def dot(left, right):
    return jnp.dot(left, right, preferred_element_type=jnp.float32)


def one_hot(mask):
    return jnp.where(mask, 1.0, 0.0).astype(jnp.bfloat16)


def dot_t(left, right):
    return lax.dot_general(
        left, right, (((1,), (1,)), ((), ())), preferred_element_type=jnp.float32
    )


def body_kernel(
    cuts,
    room,
    u_hbm,
    v_hbm,
    mod_hbm,
    den_hbm,
    adj_hbm,
    db_hbm,
    src_hbm,
    slot_hbm,
    u_hbm_out,
    v_hbm_out,
    k_hbm_out,
    u_out,
    v_out,
    k_out,
    u_ref,
    v_ref,
    mod_ref,
    den_ref,
    adj_ref,
    db_ref,
    src_ref,
    slot_ref,
    disp,
    vel,
    inv,
    adj,
    ker,
    wmod,
    acc,
    records,
    puts,
    flat,
    req,
    req_in,
    rep,
    rep_in,
    den_in,
    face_out,
    face_in,
    load_sem,
    store_sem,
    req_send,
    req_recv,
    rep_send,
    rep_recv,
    late_send,
    late_recv,
    den_send,
    den_recv,
    face_send,
    face_recv,
):
    group = lax.axis_index("groups")
    me = lax.axis_index("cuts")
    has_below = me > 0
    has_above = me < cuts - 1
    below = jnp.maximum(me - 1, 0)
    above = jnp.minimum(me + 1, cuts - 1)
    faces = src_ref.shape[1]
    table = db_ref.shape[1]
    quarter = room // 4
    rows = cuts * quarter

    loads = [
        pltpu.make_async_copy(source, target, load_sem.at[i])
        for i, (source, target) in enumerate(
            (
                (src_hbm, src_ref),
                (slot_hbm, slot_ref),
                (den_hbm, den_ref),
                (db_hbm, db_ref),
                (mod_hbm, mod_ref),
                (u_hbm, u_ref),
                (adj_hbm, adj_ref),
                (v_hbm, v_ref),
            )
        )
    ]
    for load in loads:
        load.start()

    barrier = pltpu.get_barrier_semaphore()

    def greet(k, carry):
        pl.semaphore_signal(
            barrier, inc=1, device_id=(group, lax.rem(me + k, cuts)), device_id_type=MESH
        )
        return carry

    lax.fori_loop(1, cuts, greet, 0)

    @pl.when(jnp.logical_not(has_below))
    def _():
        face_in[:, 0] = jnp.zeros((STEPS, 25, 4, 128), jnp.float32)
        den_in[0] = jnp.zeros((2, 128), jnp.float32)

    @pl.when(jnp.logical_not(has_above))
    def _():
        face_in[:, 1] = jnp.zeros((STEPS, 25, 4, 128), jnp.float32)
        den_in[1] = jnp.zeros((2, 128), jnp.float32)

    loads[0].wait()
    loads[1].wait()
    target_row = src_ref[...]
    slot_row = slot_ref[...].astype(jnp.float32)
    row_id, col_id = iota((faces, faces), 0), iota((faces, faces), 1)
    eye = row_id == col_id
    target_col = jnp.sum(jnp.where(eye, target_row, 0), axis=1, keepdims=True)
    slot_col = jnp.sum(jnp.where(eye, slot_row, 0.0), axis=1, keepdims=True)
    same = target_col == target_row
    rank_col = jnp.sum(jnp.where(same & (col_id < row_id), 1, 0), axis=1, keepdims=True)
    to_target = one_hot(iota((cuts, faces), 0) == target_row)
    at_rank = jnp.where(iota((faces, 128), 1) == rank_col, slot_col, 0.0)
    high, low = split(at_rank)
    wanted = dot(to_target, high) + dot(to_target, low)
    for peer in range(cuts):
        req[peer] = wanted[peer : peer + 1]
    loads[2].wait()

    pl.semaphore_wait(barrier, cuts - 1)

    def req_copy(k):
        peer = lax.rem(me + k, cuts)
        return pltpu.make_async_remote_copy(
            src_ref=req.at[peer],
            dst_ref=req_in.at[me],
            send_sem=req_send.at[k],
            recv_sem=req_recv.at[k],
            device_id=(group, peer),
            device_id_type=MESH,
        )

    def rep_copy(k):
        peer = lax.rem(me + k, cuts)
        return pltpu.make_async_remote_copy(
            src_ref=rep.at[peer, 0],
            dst_ref=rep_in.at[me, 0],
            send_sem=rep_send.at[k],
            recv_sem=rep_recv.at[k],
            device_id=(group, peer),
            device_id_type=MESH,
        )

    def late_copy(k):
        peer = lax.rem(me + k, cuts)
        return pltpu.make_async_remote_copy(
            src_ref=rep.at[peer, pl.ds(1, STEPS - 1)],
            dst_ref=rep_in.at[me, pl.ds(1, STEPS - 1)],
            send_sem=late_send.at[k],
            recv_sem=late_recv.at[k],
            device_id=(group, peer),
            device_id_type=MESH,
        )

    def den_copy(up):
        return pltpu.make_async_remote_copy(
            src_ref=den_ref,
            dst_ref=den_in.at[1 - up],
            send_sem=den_send.at[up],
            recv_sem=den_recv.at[up],
            device_id=(group, above if up else below),
            device_id_type=MESH,
        )

    def face_copy(step, up):
        return pltpu.make_async_remote_copy(
            src_ref=face_out.at[step, up],
            dst_ref=face_in.at[step, 1 - up],
            send_sem=face_send.at[step, up],
            recv_sem=face_recv.at[step, up],
            device_id=(group, above if up else below),
            device_id_type=MESH,
        )

    def start_all(make):
        def go(k, carry):
            make(k).start()
            return carry

        lax.fori_loop(1, cuts, go, 0)

    def wait_in(make):
        def go(k, carry):
            make(k).wait_recv()
            return carry

        lax.fori_loop(1, cuts, go, 0)

    def wait_out(make):
        def go(k, carry):
            make(k).wait_send()
            return carry

        lax.fori_loop(1, cuts, go, 0)

    start_all(req_copy)

    @pl.when(has_above)
    def _():
        den_copy(1).start()

    @pl.when(has_below)
    def _():
        den_copy(0).start()

    req_in[pl.ds(me, 1)] = req[pl.ds(me, 1)]

    place_col = (rank_col // quarter) * rows + target_col * quarter + rank_col % quarter
    element = iota((faces, EDGE * EDGE), 1)
    face_id = iota((faces, EDGE * EDGE), 0)
    line, column = element // EDGE, element % EDGE
    spots = (
        (column == 0, line),
        (column == EDGE - 1, line),
        (line == 0, column),
        (line == EDGE - 1, column),
    )
    for side, (here, along) in enumerate(spots):
        chosen = here & (face_id == along + side * EDGE)
        place = jnp.sum(jnp.where(chosen, place_col + 1, 0), axis=0, keepdims=True) - 1
        puts[side] = one_hot(iota((cuts * room, EDGE * EDGE), 0) == place)
    loads[3].wait()
    high, low = split(db_ref[...])
    disp[:, 4:8, :] = jnp.zeros((125, 4, 128), jnp.float32)
    vel[:, 4:8, :] = jnp.zeros((125, 4, 128), jnp.float32)
    adj[...] = jnp.zeros((125, 8, 128), jnp.float32)
    ker[...] = jnp.zeros((125, 8, 128), jnp.float32)
    records[...] = jnp.zeros_like(records)
    loads[4].wait()
    loads[5].wait()
    disp[:, 0:2, :] = u_ref[0]
    disp[:, 2:4, :] = u_ref[1]
    wmod[...] = weighted(jnp.concatenate([mod_ref[...]] * 4, axis=0)).reshape(25, 8, 128)

    wait_in(req_copy)
    asking = split(jnp.concatenate([req_in[s] for s in range(cuts)], axis=0))
    spread = one_hot(iota((rows, cuts), 0) // quarter == iota((rows, cuts), 1))
    repeated = dot(spread, asking[0]) + dot(spread, asking[1])
    repeated = jnp.concatenate([repeated] * 4, axis=0)
    spot = iota(repeated.shape, 0)
    spot = quarter * (spot // rows) + spot % quarter
    asked = split(jnp.where(iota(repeated.shape, 1) == spot, repeated, 0.0))
    ones = jnp.ones((128, 128), jnp.bfloat16)
    asked = (dot(asked[0], ones) + dot(asked[1], ones) + 0.5).astype(jnp.int32)
    pick = jnp.concatenate(
        [one_hot(asked == iota(asked.shape, 1) + at) for at in range(0, table, 128)], axis=1
    )
    served = dot_t(pick, high) + dot_t(pick, low)
    served = jnp.concatenate([served, jnp.zeros((4 * rows, 128 - served.shape[1]), jnp.float32)], axis=1)
    lane = iota((rows, 128), 1)

    def lay_out(step):
        packed = None
        for j in range(4):
            moved = pltpu.roll(served[j * rows : (j + 1) * rows], (32 * j - 25 * step) % 128, 1)
            packed = moved if j == 0 else jnp.where(lane < 32 * j, packed, moved)
        for peer in range(cuts):
            rep[peer, step] = packed[peer * quarter : (peer + 1) * quarter]

    lay_out(0)
    start_all(rep_copy)
    for step in range(1, STEPS):
        lay_out(step)
    start_all(late_copy)
    rep_in[pl.ds(me, 1)] = rep[pl.ds(me, 1)]

    loads[6].wait()
    loads[7].wait()
    vel[:, 0:2, :] = v_ref[0]
    vel[:, 2:4, :] = v_ref[1]
    adj[:, 2:4, :] = adj_ref[...]

    @pl.when(has_below)
    def _():
        den_copy(1).wait_recv()

    @pl.when(has_above)
    def _():
        den_copy(0).wait_recv()

    density = jnp.concatenate([den_ref[...]] * 4, axis=0)
    for a in range(5):
        if a in (0, 1, 4):
            near = density
            if a != 1:
                near = near + jnp.concatenate([den_in[a // 4]] * 4, axis=0)
            mass = join_plane(weighted(near)).reshape(25, 8, 128)
            base = TIME_STEP / mass
        inv[25 * a : 25 * a + 25] = float(1.0 / WEIGHTS[a]) * base

    node = iota((128, 1), 0) % 32

    def weight_of(index):
        return jnp.where(
            (index == 0) | (index == 4),
            float(WEIGHTS[0]),
            jnp.where(index == 2, float(WEIGHTS[2]), float(WEIGHTS[1])),
        )

    face_weight = weight_of(node // 5) * weight_of(node % 5)

    def place_records(first, last):
        for step in range(first, last):
            for s in range(cuts):
                flat[step, s * quarter : (s + 1) * quarter] = rep_in[s, step]
        parts = []
        for j in range(4):
            part = None
            for step in range(first, last):
                moved = pltpu.roll(flat[step], (32 * (step - j)) % 128, 1)
                part = moved if part is None else jnp.where(lane < 32 * step, part, moved)
            parts.append(part)
        got = jnp.transpose(jnp.concatenate(parts, axis=0)) * face_weight
        got = got[32 * first : 32 * last]
        count = got.shape[0]
        got = jnp.concatenate(split(got), axis=0)
        for side in range(4):
            moved = dot(got, puts[side])
            moved = moved[0:count] + moved[count:]
            at = slice(32 * first, 32 * last)
            records[side, at, 0, :] = moved[:, 0:128]
            records[side, at, 1, :] = moved[:, 128:256]

    def plane_of(ref, a):
        return ref[25 * a : 25 * a + 25].reshape(5, 5, 8, 128)

    def stiff(a):
        plane = plane_of(disp, a)
        total = mix(STIFF[a], [plane_of(disp, k) for k in range(5)])
        coupling = STIFF_W * WEIGHTS[a]
        total = total + jnp.stack([mix(coupling[b], [plane[k] for k in range(5)]) for b in range(5)])
        total = total + jnp.stack(
            [mix(coupling[c], [plane[:, k] for k in range(5)]) for c in range(5)], axis=1
        )
        return plane_of(adj, a) - wmod[...].reshape(5, 5, 8, 128) * total

    def joined(step, a, force):
        at = pl.ds(32 * step + 5 * a, 5)
        force = jnp.concatenate(
            [
                (force[:, 0] + records[0, at])[:, None],
                force[:, 1:4],
                (force[:, 4] + records[1, at])[:, None],
            ],
            axis=1,
        )
        force = jnp.concatenate(
            [
                (force[0] + records[2, at])[None],
                force[1:4],
                (force[4] + records[3, at])[None],
            ],
            axis=0,
        )
        return join_plane(force).reshape(25, 8, 128)

    def advance(a, force):
        rows = slice(25 * a, 25 * a + 25)
        speed = vel[rows] + inv[rows] * force
        vel[rows] = speed
        disp[rows] = disp[rows] + TIME_STEP * speed

    def sensitivity(a):
        plane = plane_of(disp, a)
        total = 0.0
        for grad in (
            mix(DERIV[a], [plane_of(disp, k) for k in range(5)]),
            jnp.stack([mix(DERIV[b], [plane[k] for k in range(5)]) for b in range(5)]),
            jnp.stack([mix(DERIV[c], [plane[:, k] for k in range(5)]) for c in range(5)], axis=1),
        ):
            grad = grad.reshape(25, 8, 128)
            total = total + grad * pltpu.roll(grad, 6, 1)
        rows = slice(25 * a, 25 * a + 25)
        ker[rows] = ker[rows] + total

    def one_step(step, first):
        for a in (4, 0):
            force = joined(step, a, plane_of(acc, a) if first else stiff(a))
            acc[25 * a : 25 * a + 25] = force
            face_out[step, a // 4] = force[:, 0:4]
            if a:

                @pl.when(has_above)
                def _():
                    face_copy(step, 1).start()
            else:

                @pl.when(has_below)
                def _():
                    face_copy(step, 0).start()

        for a in (1, 2, 3):
            acc[25 * a : 25 * a + 25] = joined(step, a, plane_of(acc, a) if first else stiff(a))
        if not first:
            for a in range(5):
                sensitivity(a)
        for a in (1, 2, 3):
            advance(a, acc[25 * a : 25 * a + 25])
        if first:
            wait_in(late_copy)
            place_records(1, STEPS)

        @pl.when(has_below)
        def _():
            face_copy(step, 1).wait_recv()

        @pl.when(has_above)
        def _():
            face_copy(step, 0).wait_recv()

        for a in (0, 4):
            other = face_in[step, a // 4]
            other = jnp.concatenate([other, jnp.zeros_like(other)], axis=1)
            advance(a, acc[25 * a : 25 * a + 25] + other)

        @pl.when(has_above)
        def _():
            face_copy(step, 1).wait_send()

        @pl.when(has_below)
        def _():
            face_copy(step, 0).wait_send()

    for a in range(5):
        acc[25 * a : 25 * a + 25] = stiff(a).reshape(25, 8, 128)
    for a in range(5):
        sensitivity(a)
    wait_in(rep_copy)
    place_records(0, 1)
    one_step(0, True)

    def later(step, carry):
        one_step(step, False)
        return carry

    lax.fori_loop(1, STEPS, later, 0)

    stores = [
        pltpu.make_async_copy(source, target, store_sem.at[i])
        for i, (source, target) in enumerate(
            ((u_out, u_hbm_out), (v_out, v_hbm_out), (k_out, k_hbm_out))
        )
    ]
    for field in range(2):
        u_out[field] = disp[:, 2 * field : 2 * field + 2, :]
    stores[0].start()
    for field in range(2):
        v_out[field] = vel[:, 2 * field : 2 * field + 2, :]
    stores[1].start()
    k_out[...] = ker[:, 0:2, :] * (-TIME_STEP * mod_ref[...])
    stores[2].start()
    for make in (req_copy, rep_copy, late_copy):
        wait_out(make)

    @pl.when(has_above)
    def _():
        den_copy(1).wait_send()

    @pl.when(has_below)
    def _():
        den_copy(0).wait_send()

    for store in stores:
        store.wait()


def store_kernel(u_in, v_in, k_in, u_out, v_out, k_out, u_held, v_held, k_held, sems):
    held = (u_held, v_held, k_held)
    inward = [
        pltpu.make_async_copy(source, target, sems.at[i])
        for i, (source, target) in enumerate(zip((u_in, v_in, k_in), held))
    ]
    outward = [
        pltpu.make_async_copy(source, target, sems.at[3 + i])
        for i, (source, target) in enumerate(zip(held, (u_out, v_out, k_out)))
    ]
    for copy in inward:
        copy.start()
    for copy, onward in zip(inward, outward):
        copy.wait()
        onward.start()
    for copy in outward:
        copy.wait()


def body(
    displacement, velocity, modulus, density, adjoint_source, database, face_source, face_slot
):
    cuts = lax.axis_size("cuts")
    faces = face_source.shape[0]
    capacity = max(2, 4 * faces // cuts)
    room = -(-capacity // 4) * 4
    quarter = room // 4
    vmem = pl.BlockSpec(memory_space=pltpu.VMEM)
    hbm = pl.BlockSpec(memory_space=pl.ANY)
    f32 = jnp.float32
    dma = pltpu.SemaphoreType.DMA
    big = pltpu.VMEM((125, 8, 128), f32)
    shapes = (
        jax.ShapeDtypeStruct((2, 125, 2, 128), f32),
        jax.ShapeDtypeStruct((2, 125, 2, 128), f32),
        jax.ShapeDtypeStruct((125, 2, 128), f32),
    )
    operands = (
        displacement.reshape(2, 125, 2, 128),
        velocity.reshape(2, 125, 2, 128),
        modulus.reshape(2, 128),
        density.reshape(2, 128),
        adjoint_source.reshape(125, 2, 128),
        database.T,
        face_source.reshape(1, faces),
        face_slot.reshape(1, faces),
    )
    out = pl.pallas_call(
        functools.partial(body_kernel, cuts, room),
        out_shape=shapes,
        in_specs=[hbm] * 8,
        out_specs=(hbm, hbm, hbm),
        scratch_shapes=[pltpu.VMEM(x.shape, x.dtype) for x in shapes + operands]
        + [
            big,
            big,
            big,
            big,
            big,
            pltpu.VMEM((25, 8, 128), f32),
            big,
            pltpu.VMEM((4, 128, 8, 128), f32),
            pltpu.VMEM((4, cuts * room, EDGE * EDGE), jnp.bfloat16),
            pltpu.VMEM((STEPS, cuts * quarter, 128), f32),
            pltpu.VMEM((cuts, 1, 128), f32),
            pltpu.VMEM((cuts, 1, 128), f32),
            pltpu.VMEM((cuts, STEPS, quarter, 128), f32),
            pltpu.VMEM((cuts, STEPS, quarter, 128), f32),
            pltpu.VMEM((2, 2, 128), f32),
            pltpu.VMEM((STEPS, 2, 25, 4, 128), f32),
            pltpu.VMEM((STEPS, 2, 25, 4, 128), f32),
            dma((8,)),
            dma((3,)),
            dma((cuts,)),
            dma((cuts,)),
            dma((cuts,)),
            dma((cuts,)),
            dma((cuts,)),
            dma((cuts,)),
            dma((2,)),
            dma((2,)),
            dma((STEPS, 2)),
            dma((STEPS, 2)),
        ],
        compiler_params=pltpu.CompilerParams(
            collective_id=0, has_side_effects=True, vmem_limit_bytes=63 * 1024 * 1024
        ),
    )(*operands)
    out = pl.pallas_call(
        store_kernel,
        out_shape=shapes,
        in_specs=[hbm] * 3,
        out_specs=(hbm, hbm, hbm),
        scratch_shapes=[pltpu.VMEM(x.shape, x.dtype) for x in shapes] + [dma((6,))],
        compiler_params=pltpu.CompilerParams(vmem_limit_bytes=63 * 1024 * 1024),
    )(*out)
    return (
        out[0].reshape(displacement.shape),
        out[1].reshape(velocity.shape),
        out[2].reshape(adjoint_source.shape),
    )


def solution(mesh):
    return jax.shard_map(
        body,
        mesh=mesh,
        in_specs=(
            P(None, None, None, None, ("groups", "cuts"), None),
            P(None, None, None, None, ("groups", "cuts"), None),
            P(("groups", "cuts"), None),
            P(("groups", "cuts"), None),
            P(None, None, None, ("groups", "cuts"), None),
            P(("groups", "cuts"), None),
            P(("groups", "cuts"), None),
            P(("groups", "cuts")),
        ),
        out_specs=(
            P(None, None, None, None, ("groups", "cuts"), None),
            P(None, None, None, None, ("groups", "cuts"), None),
            P(None, None, None, ("groups", "cuts"), None),
        ),
        check_vma=False,
    )
```

```python
import functools
import math

import jax
import jax.numpy as jnp
import numpy as np
from jax import lax
from jax.experimental import pallas as pl
from jax.experimental.pallas import tpu as pltpu
from jax.sharding import PartitionSpec as P

EDGE = 16
STEPS = 4
TIME_STEP = 0.03
MESH = pl.DeviceIdType.MESH


def gll_tables():
    points = np.array([-1.0, -math.sqrt(3.0 / 7.0), 0.0, math.sqrt(3.0 / 7.0), 1.0])
    weights = np.array([0.1, 49.0 / 90.0, 32.0 / 45.0, 49.0 / 90.0, 0.1])
    derivative = np.zeros((5, 5))
    for node_row in range(5):
        for node_col in range(5):
            summed = 0.0
            for other_node in range(5):
                if other_node == node_col:
                    continue
                term = 1.0 / (points[node_col] - points[other_node])
                for third_node in range(5):
                    if third_node != node_col and third_node != other_node:
                        term = (
                            term
                            * (points[node_row] - points[third_node])
                            / (points[node_col] - points[third_node])
                        )
                summed = summed + term
            derivative[node_row, node_col] = summed
    return (derivative, weights)


DERIV, WEIGHTS = gll_tables()
STIFF = DERIV.T @ np.diag(WEIGHTS) @ DERIV
STIFF_W = STIFF / WEIGHTS[:, None]


def mix(row, parts):
    total = None
    for coefficient, part in zip(row, parts):
        if abs(coefficient) < 1e-12:
            continue
        term = float(coefficient) * part
        total = term if total is None else total + term
    return total


def iota(shape, dim):
    return lax.broadcasted_iota(jnp.int32, shape, dim)


def join_plane(plane):
    lane = iota((8, 128), 1)
    half = iota((8, 128), 0) % 2
    column = lane % EDGE
    first, last = plane[:, 0], plane[:, 4]
    from_left = jnp.where(column != 0, pltpu.roll(last, 1, 2), 0.0)
    from_right = jnp.where(column != EDGE - 1, pltpu.roll(first, 127, 2), 0.0)
    plane = jnp.concatenate(
        [(first + from_left)[:, None], plane[:, 1:4], (last + from_right)[:, None]], axis=1
    )
    first, last = plane[0], plane[4]
    rolled = pltpu.roll(last, EDGE, 2)
    under = jnp.where(half != 0, pltpu.roll(rolled, 1, 1), 0.0)
    from_left = jnp.where(lane < EDGE, under, rolled)
    rolled = pltpu.roll(first, 128 - EDGE, 2)
    over = jnp.where(half == 0, pltpu.roll(rolled, 7, 1), 0.0)
    from_right = jnp.where(lane >= 128 - EDGE, over, rolled)
    return jnp.concatenate(
        [(first + from_left)[None], plane[1:4], (last + from_right)[None]], axis=0
    )


def weighted(values):
    rows = [
        jnp.stack([float(WEIGHTS[b] * WEIGHTS[c]) * values for c in range(5)]) for b in range(5)
    ]
    return jnp.stack(rows)


def split(values):
    high = values.astype(jnp.bfloat16)
    low = (values - high.astype(jnp.float32)).astype(jnp.bfloat16)
    return high, low


def dot(left, right):
    return jnp.dot(left, right, preferred_element_type=jnp.float32)


def one_hot(mask):
    return jnp.where(mask, 1.0, 0.0).astype(jnp.bfloat16)


def dot_t(left, right):
    return lax.dot_general(
        left, right, (((1,), (1,)), ((), ())), preferred_element_type=jnp.float32
    )


def body_kernel(
    cuts,
    room,
    u_hbm,
    v_hbm,
    mod_hbm,
    den_hbm,
    adj_hbm,
    db_hbm,
    src_hbm,
    slot_hbm,
    u_hbm_out,
    v_hbm_out,
    k_hbm_out,
    u_out,
    v_out,
    k_out,
    u_ref,
    v_ref,
    mod_ref,
    den_ref,
    adj_ref,
    db_ref,
    src_ref,
    slot_ref,
    disp,
    vel,
    inv,
    adj,
    ker,
    wmod,
    acc,
    records,
    puts,
    flat,
    req,
    req_in,
    rep,
    rep_in,
    den_in,
    face_out,
    face_in,
    load_sem,
    store_sem,
    req_send,
    req_recv,
    rep_send,
    rep_recv,
    late_send,
    late_recv,
    den_send,
    den_recv,
    face_send,
    face_recv,
):
    group = lax.axis_index("groups")
    me = lax.axis_index("cuts")
    has_below = me > 0
    has_above = me < cuts - 1
    below = jnp.maximum(me - 1, 0)
    above = jnp.minimum(me + 1, cuts - 1)
    faces = src_ref.shape[1]
    table = db_ref.shape[1]
    quarter = room // 4
    rows = cuts * quarter

    loads = [
        pltpu.make_async_copy(source, target, load_sem.at[i])
        for i, (source, target) in enumerate(
            (
                (src_hbm, src_ref),
                (slot_hbm, slot_ref),
                (den_hbm, den_ref),
                (db_hbm, db_ref),
                (mod_hbm, mod_ref),
                (u_hbm, u_ref),
                (adj_hbm, adj_ref),
                (v_hbm, v_ref),
            )
        )
    ]
    for load in loads:
        load.start()

    barrier = pltpu.get_barrier_semaphore()

    def greet(k, carry):
        pl.semaphore_signal(
            barrier, inc=1, device_id=(group, lax.rem(me + k, cuts)), device_id_type=MESH
        )
        return carry

    lax.fori_loop(1, cuts, greet, 0)

    @pl.when(jnp.logical_not(has_below))
    def _():
        face_in[:, 0] = jnp.zeros((STEPS, 25, 4, 128), jnp.float32)
        den_in[0] = jnp.zeros((2, 128), jnp.float32)

    @pl.when(jnp.logical_not(has_above))
    def _():
        face_in[:, 1] = jnp.zeros((STEPS, 25, 4, 128), jnp.float32)
        den_in[1] = jnp.zeros((2, 128), jnp.float32)

    loads[0].wait()
    loads[1].wait()
    target_row = src_ref[...]
    slot_row = slot_ref[...].astype(jnp.float32)
    row_id, col_id = iota((faces, faces), 0), iota((faces, faces), 1)
    eye = row_id == col_id
    target_col = jnp.sum(jnp.where(eye, target_row, 0), axis=1, keepdims=True)
    slot_col = jnp.sum(jnp.where(eye, slot_row, 0.0), axis=1, keepdims=True)
    same = target_col == target_row
    rank_col = jnp.sum(jnp.where(same & (col_id < row_id), 1, 0), axis=1, keepdims=True)
    to_target = one_hot(iota((cuts, faces), 0) == target_row)
    at_rank = jnp.where(iota((faces, 128), 1) == rank_col, slot_col, 0.0)
    high, low = split(at_rank)
    wanted = dot(to_target, high) + dot(to_target, low)
    for peer in range(cuts):
        req[peer] = wanted[peer : peer + 1]
    loads[2].wait()

    pl.semaphore_wait(barrier, cuts - 1)

    def req_copy(k):
        peer = lax.rem(me + k, cuts)
        return pltpu.make_async_remote_copy(
            src_ref=req.at[peer],
            dst_ref=req_in.at[me],
            send_sem=req_send.at[k],
            recv_sem=req_recv.at[k],
            device_id=(group, peer),
            device_id_type=MESH,
        )

    def rep_copy(k):
        peer = lax.rem(me + k, cuts)
        return pltpu.make_async_remote_copy(
            src_ref=rep.at[peer, 0],
            dst_ref=rep_in.at[me, 0],
            send_sem=rep_send.at[k],
            recv_sem=rep_recv.at[k],
            device_id=(group, peer),
            device_id_type=MESH,
        )

    def late_copy(k):
        peer = lax.rem(me + k, cuts)
        return pltpu.make_async_remote_copy(
            src_ref=rep.at[peer, pl.ds(1, STEPS - 1)],
            dst_ref=rep_in.at[me, pl.ds(1, STEPS - 1)],
            send_sem=late_send.at[k],
            recv_sem=late_recv.at[k],
            device_id=(group, peer),
            device_id_type=MESH,
        )

    def den_copy(up):
        return pltpu.make_async_remote_copy(
            src_ref=den_ref,
            dst_ref=den_in.at[1 - up],
            send_sem=den_send.at[up],
            recv_sem=den_recv.at[up],
            device_id=(group, above if up else below),
            device_id_type=MESH,
        )

    def face_copy(step, up):
        return pltpu.make_async_remote_copy(
            src_ref=face_out.at[step, up],
            dst_ref=face_in.at[step, 1 - up],
            send_sem=face_send.at[step, up],
            recv_sem=face_recv.at[step, up],
            device_id=(group, above if up else below),
            device_id_type=MESH,
        )

    def start_all(make):
        def go(k, carry):
            make(k).start()
            return carry

        lax.fori_loop(1, cuts, go, 0)

    def wait_in(make):
        def go(k, carry):
            make(k).wait_recv()
            return carry

        lax.fori_loop(1, cuts, go, 0)

    def wait_out(make):
        def go(k, carry):
            make(k).wait_send()
            return carry

        lax.fori_loop(1, cuts, go, 0)

    start_all(req_copy)

    @pl.when(has_above)
    def _():
        den_copy(1).start()

    @pl.when(has_below)
    def _():
        den_copy(0).start()

    req_in[pl.ds(me, 1)] = req[pl.ds(me, 1)]

    place_col = (rank_col // quarter) * rows + target_col * quarter + rank_col % quarter
    element = iota((faces, EDGE * EDGE), 1)
    face_id = iota((faces, EDGE * EDGE), 0)
    line, column = element // EDGE, element % EDGE
    spots = (
        (column == 0, line),
        (column == EDGE - 1, line),
        (line == 0, column),
        (line == EDGE - 1, column),
    )
    for side, (here, along) in enumerate(spots):
        chosen = here & (face_id == along + side * EDGE)
        place = jnp.sum(jnp.where(chosen, place_col + 1, 0), axis=0, keepdims=True) - 1
        puts[side] = one_hot(iota((cuts * room, EDGE * EDGE), 0) == place)
    loads[3].wait()
    high, low = split(db_ref[...])
    disp[:, 4:8, :] = jnp.zeros((125, 4, 128), jnp.float32)
    vel[:, 4:8, :] = jnp.zeros((125, 4, 128), jnp.float32)
    adj[...] = jnp.zeros((125, 8, 128), jnp.float32)
    ker[...] = jnp.zeros((125, 8, 128), jnp.float32)
    records[...] = jnp.zeros_like(records)
    loads[4].wait()
    loads[5].wait()
    disp[:, 0:2, :] = u_ref[0]
    disp[:, 2:4, :] = u_ref[1]
    wmod[...] = weighted(jnp.concatenate([mod_ref[...]] * 4, axis=0)).reshape(25, 8, 128)

    wait_in(req_copy)
    asking = split(jnp.concatenate([req_in[s] for s in range(cuts)], axis=0))
    spread = one_hot(iota((rows, cuts), 0) // quarter == iota((rows, cuts), 1))
    repeated = dot(spread, asking[0]) + dot(spread, asking[1])
    repeated = jnp.concatenate([repeated] * 4, axis=0)
    spot = iota(repeated.shape, 0)
    spot = quarter * (spot // rows) + spot % quarter
    asked = split(jnp.where(iota(repeated.shape, 1) == spot, repeated, 0.0))
    ones = jnp.ones((128, 128), jnp.bfloat16)
    asked = (dot(asked[0], ones) + dot(asked[1], ones) + 0.5).astype(jnp.int32)
    pick = jnp.concatenate(
        [one_hot(asked == iota(asked.shape, 1) + at) for at in range(0, table, 128)], axis=1
    )
    served = dot_t(pick, high) + dot_t(pick, low)
    served = jnp.concatenate([served, jnp.zeros((4 * rows, 128 - served.shape[1]), jnp.float32)], axis=1)
    lane = iota((rows, 128), 1)

    def lay_out(step):
        packed = None
        for j in range(4):
            moved = pltpu.roll(served[j * rows : (j + 1) * rows], (32 * j - 25 * step) % 128, 1)
            packed = moved if j == 0 else jnp.where(lane < 32 * j, packed, moved)
        for peer in range(cuts):
            rep[peer, step] = packed[peer * quarter : (peer + 1) * quarter]

    lay_out(0)
    start_all(rep_copy)
    for step in range(1, STEPS):
        lay_out(step)
    start_all(late_copy)
    rep_in[pl.ds(me, 1)] = rep[pl.ds(me, 1)]

    loads[6].wait()
    loads[7].wait()
    vel[:, 0:2, :] = v_ref[0]
    vel[:, 2:4, :] = v_ref[1]
    adj[:, 2:4, :] = adj_ref[...]

    @pl.when(has_below)
    def _():
        den_copy(1).wait_recv()

    @pl.when(has_above)
    def _():
        den_copy(0).wait_recv()

    density = jnp.concatenate([den_ref[...]] * 4, axis=0)
    for a in range(5):
        if a in (0, 1, 4):
            near = density
            if a != 1:
                near = near + jnp.concatenate([den_in[a // 4]] * 4, axis=0)
            mass = join_plane(weighted(near)).reshape(25, 8, 128)
            base = TIME_STEP / mass
        inv[25 * a : 25 * a + 25] = float(1.0 / WEIGHTS[a]) * base

    node = iota((128, 1), 0) % 32

    def weight_of(index):
        return jnp.where(
            (index == 0) | (index == 4),
            float(WEIGHTS[0]),
            jnp.where(index == 2, float(WEIGHTS[2]), float(WEIGHTS[1])),
        )

    face_weight = weight_of(node // 5) * weight_of(node % 5)

    def place_records(first, last):
        for step in range(first, last):
            for s in range(cuts):
                flat[step, s * quarter : (s + 1) * quarter] = rep_in[s, step]
        parts = []
        for j in range(4):
            part = None
            for step in range(first, last):
                moved = pltpu.roll(flat[step], (32 * (step - j)) % 128, 1)
                part = moved if part is None else jnp.where(lane < 32 * step, part, moved)
            parts.append(part)
        got = jnp.transpose(jnp.concatenate(parts, axis=0)) * face_weight
        got = got[32 * first : 32 * last]
        count = got.shape[0]
        got = jnp.concatenate(split(got), axis=0)
        for side in range(4):
            moved = dot(got, puts[side])
            moved = moved[0:count] + moved[count:]
            at = slice(32 * first, 32 * last)
            records[side, at, 0, :] = moved[:, 0:128]
            records[side, at, 1, :] = moved[:, 128:256]

    def plane_of(ref, a):
        return ref[25 * a : 25 * a + 25].reshape(5, 5, 8, 128)

    def stiff(a):
        plane = plane_of(disp, a)
        total = mix(STIFF[a], [plane_of(disp, k) for k in range(5)])
        coupling = STIFF_W * WEIGHTS[a]
        total = total + jnp.stack([mix(coupling[b], [plane[k] for k in range(5)]) for b in range(5)])
        total = total + jnp.stack(
            [mix(coupling[c], [plane[:, k] for k in range(5)]) for c in range(5)], axis=1
        )
        return plane_of(adj, a) - wmod[...].reshape(5, 5, 8, 128) * total

    def joined(step, a, force):
        at = pl.ds(32 * step + 5 * a, 5)
        force = jnp.concatenate(
            [
                (force[:, 0] + records[0, at])[:, None],
                force[:, 1:4],
                (force[:, 4] + records[1, at])[:, None],
            ],
            axis=1,
        )
        force = jnp.concatenate(
            [
                (force[0] + records[2, at])[None],
                force[1:4],
                (force[4] + records[3, at])[None],
            ],
            axis=0,
        )
        return join_plane(force).reshape(25, 8, 128)

    def advance(a, force):
        rows = slice(25 * a, 25 * a + 25)
        speed = vel[rows] + inv[rows] * force
        vel[rows] = speed
        disp[rows] = disp[rows] + TIME_STEP * speed

    def sensitivity(a):
        plane = plane_of(disp, a)
        total = 0.0
        for grad in (
            mix(DERIV[a], [plane_of(disp, k) for k in range(5)]),
            jnp.stack([mix(DERIV[b], [plane[k] for k in range(5)]) for b in range(5)]),
            jnp.stack([mix(DERIV[c], [plane[:, k] for k in range(5)]) for c in range(5)], axis=1),
        ):
            grad = grad.reshape(25, 8, 128)
            total = total + grad * pltpu.roll(grad, 6, 1)
        rows = slice(25 * a, 25 * a + 25)
        ker[rows] = ker[rows] + total

    stores = []

    def store(source, target):
        copy = pltpu.make_async_copy(source, target, store_sem.at[len(stores)])
        copy.start()
        stores.append(copy)

    def give(low_row, high_row):
        rows = slice(low_row, high_row)
        at = pl.ds(low_row, high_row - low_row)
        for field in range(2):
            u_out[field, rows] = disp[rows, 2 * field : 2 * field + 2, :]
            store(u_out.at[field, at], u_hbm_out.at[field, at])
            v_out[field, rows] = vel[rows, 2 * field : 2 * field + 2, :]
            store(v_out.at[field, at], v_hbm_out.at[field, at])

    def give_kernel():
        k_out[...] = ker[:, 0:2, :] * (-TIME_STEP * mod_ref[...])
        store(k_out, k_hbm_out)

    def one_step(step, first, last):
        for a in (4, 0):
            force = joined(step, a, plane_of(acc, a) if first else stiff(a))
            acc[25 * a : 25 * a + 25] = force
            face_out[step, a // 4] = force[:, 0:4]
            if a:

                @pl.when(has_above)
                def _():
                    face_copy(step, 1).start()
            else:

                @pl.when(has_below)
                def _():
                    face_copy(step, 0).start()

        for a in (1, 2, 3):
            acc[25 * a : 25 * a + 25] = joined(step, a, plane_of(acc, a) if first else stiff(a))
        if not first:
            for a in range(5):
                sensitivity(a)
        for a in (1, 2, 3):
            advance(a, acc[25 * a : 25 * a + 25])
        if first:
            wait_in(late_copy)
            place_records(1, STEPS)
        if last:
            give_kernel()
            give(25, 100)

        @pl.when(has_below)
        def _():
            face_copy(step, 1).wait_recv()

        @pl.when(has_above)
        def _():
            face_copy(step, 0).wait_recv()

        for a in (0, 4):
            other = face_in[step, a // 4]
            other = jnp.concatenate([other, jnp.zeros_like(other)], axis=1)
            advance(a, acc[25 * a : 25 * a + 25] + other)

    for a in range(5):
        acc[25 * a : 25 * a + 25] = stiff(a).reshape(25, 8, 128)
    for a in range(5):
        sensitivity(a)
    wait_in(rep_copy)
    place_records(0, 1)
    one_step(0, True, False)

    def later(step, carry):
        one_step(step, False, False)
        return carry

    lax.fori_loop(1, STEPS - 1, later, 0)
    one_step(STEPS - 1, False, True)
    give(0, 25)
    give(100, 125)

    def sent(k, carry):
        @pl.when(has_above)
        def _():
            face_copy(k, 1).wait_send()

        @pl.when(has_below)
        def _():
            face_copy(k, 0).wait_send()

        return carry

    lax.fori_loop(0, STEPS, sent, 0)
    for make in (req_copy, rep_copy, late_copy):
        wait_out(make)

    @pl.when(has_above)
    def _():
        den_copy(1).wait_send()

    @pl.when(has_below)
    def _():
        den_copy(0).wait_send()

    for copy in stores:
        copy.wait()


def store_kernel(u_in, v_in, k_in, u_out, v_out, k_out, u_held, v_held, k_held, sems):
    pieces = [
        (lambda ref, field=field, at=at: ref.at[field, at], refs)
        for refs in ((u_in, u_held, u_out), (v_in, v_held, v_out))
        for field in range(2)
        for at in (pl.ds(0, 64), pl.ds(64, 61))
    ]
    pieces += [
        (lambda ref, at=at: ref.at[at], (k_in, k_held, k_out)) for at in (pl.ds(0, 64), pl.ds(64, 61))
    ]
    inward = [
        pltpu.make_async_copy(view(refs[0]), view(refs[1]), sems.at[0, i])
        for i, (view, refs) in enumerate(pieces)
    ]
    outward = [
        pltpu.make_async_copy(view(refs[1]), view(refs[2]), sems.at[1, i])
        for i, (view, refs) in enumerate(pieces)
    ]
    for copy in inward:
        copy.start()
    for copy, onward in zip(inward, outward):
        copy.wait()
        onward.start()
    for copy in outward:
        copy.wait()


def body(
    displacement, velocity, modulus, density, adjoint_source, database, face_source, face_slot
):
    cuts = lax.axis_size("cuts")
    faces = face_source.shape[0]
    capacity = max(2, 4 * faces // cuts)
    room = -(-capacity // 4) * 4
    quarter = room // 4
    vmem = pl.BlockSpec(memory_space=pltpu.VMEM)
    hbm = pl.BlockSpec(memory_space=pl.ANY)
    f32 = jnp.float32
    dma = pltpu.SemaphoreType.DMA
    big = pltpu.VMEM((125, 8, 128), f32)
    shapes = (
        jax.ShapeDtypeStruct((2, 125, 2, 128), f32),
        jax.ShapeDtypeStruct((2, 125, 2, 128), f32),
        jax.ShapeDtypeStruct((125, 2, 128), f32),
    )
    operands = (
        displacement.reshape(2, 125, 2, 128),
        velocity.reshape(2, 125, 2, 128),
        modulus.reshape(2, 128),
        density.reshape(2, 128),
        adjoint_source.reshape(125, 2, 128),
        database.T,
        face_source.reshape(1, faces),
        face_slot.reshape(1, faces),
    )
    out = pl.pallas_call(
        functools.partial(body_kernel, cuts, room),
        out_shape=shapes,
        in_specs=[hbm] * 8,
        out_specs=(hbm, hbm, hbm),
        scratch_shapes=[pltpu.VMEM(x.shape, x.dtype) for x in shapes + operands]
        + [
            big,
            big,
            big,
            big,
            big,
            pltpu.VMEM((25, 8, 128), f32),
            big,
            pltpu.VMEM((4, 128, 8, 128), f32),
            pltpu.VMEM((4, cuts * room, EDGE * EDGE), jnp.bfloat16),
            pltpu.VMEM((STEPS, cuts * quarter, 128), f32),
            pltpu.VMEM((cuts, 1, 128), f32),
            pltpu.VMEM((cuts, 1, 128), f32),
            pltpu.VMEM((cuts, STEPS, quarter, 128), f32),
            pltpu.VMEM((cuts, STEPS, quarter, 128), f32),
            pltpu.VMEM((2, 2, 128), f32),
            pltpu.VMEM((STEPS, 2, 25, 4, 128), f32),
            pltpu.VMEM((STEPS, 2, 25, 4, 128), f32),
            dma((8,)),
            dma((13,)),
            dma((cuts,)),
            dma((cuts,)),
            dma((cuts,)),
            dma((cuts,)),
            dma((cuts,)),
            dma((cuts,)),
            dma((2,)),
            dma((2,)),
            dma((STEPS, 2)),
            dma((STEPS, 2)),
        ],
        compiler_params=pltpu.CompilerParams(
            collective_id=0, has_side_effects=True, vmem_limit_bytes=63 * 1024 * 1024
        ),
    )(*operands)
    out = pl.pallas_call(
        store_kernel,
        out_shape=shapes,
        in_specs=[hbm] * 3,
        out_specs=(hbm, hbm, hbm),
        scratch_shapes=[pltpu.VMEM(x.shape, x.dtype) for x in shapes] + [dma((2, 10))],
        compiler_params=pltpu.CompilerParams(vmem_limit_bytes=63 * 1024 * 1024),
    )(*out)
    return (
        out[0].reshape(displacement.shape),
        out[1].reshape(velocity.shape),
        out[2].reshape(adjoint_source.shape),
    )


def solution(mesh):
    return jax.shard_map(
        body,
        mesh=mesh,
        in_specs=(
            P(None, None, None, None, ("groups", "cuts"), None),
            P(None, None, None, None, ("groups", "cuts"), None),
            P(("groups", "cuts"), None),
            P(("groups", "cuts"), None),
            P(None, None, None, ("groups", "cuts"), None),
            P(("groups", "cuts"), None),
            P(("groups", "cuts"), None),
            P(("groups", "cuts")),
        ),
        out_specs=(
            P(None, None, None, None, ("groups", "cuts"), None),
            P(None, None, None, None, ("groups", "cuts"), None),
            P(None, None, None, ("groups", "cuts"), None),
        ),
        check_vma=False,
    )
```
